512 devices in a mesh: ctx: 32 (over y_hi, z), tp: 16 (over y_lo, x, core).
Axes of the slice: x: 4, y: 8 (y_hi: 4, y_lo: 2; y = y_hi * 2 + y_lo), z: 8, core: 2. Of those that a mesh axis runs over, the one named last changes fastest.
Arguments:
- queries: bfloat16 [4096, 8192], P('ctx', 'tp'), may hold values from -56 to 56
- suffix_kv: bfloat16 [2, 4096, 2048], P(None, 'ctx', 'tp'), may hold values from -6 to 6
- cache_pool: bfloat16 [2, 512, 128, 2048], P(None, 'ctx', None, 'tp'), may hold values from -6 to 6
- hit_count: int32 [32], replicated, may hold values from 1 to 3, as said below
- hit_slots: int32 [32, 3], P('ctx'), may hold values from 0 to 15, as said below
- out_weight: bfloat16 [8192, 8192], P('tp', 'ctx'), may hold values from -1.1953125 to 1.1953125
Outputs:
- layer_out: bfloat16 [4096, 8192], P('tp', 'ctx')
The draws below stay inside these ranges and needn't reach their ends.
Inputs may be any that keep to these rules, and one draw needn't show every extreme that they name: hit_count[h] blocks of holder h belong to the prefix; some holder has exactly 3. `hit_slots`: row h names 3 distinct slots of holder h's pool; only its first hit_count[h] entries are hits, the others are unused.
All inputs are finite; a program needn't handle non-finite values.
Results may differ from the reference program's by a relative error of at most 0.024.
Values may be sent and summed in bfloat16 or wider, within the bound.
A program may use at most 64 MiB of HBM per device.

```python
import math
import jax
import jax.numpy as jnp
from jax import lax

D = 8192
HQ = 64
HD = 128
BLK = 128
HCAP = 3
HOLD = 16
SLOTS = 16
SPAN = 4096
N_CTX = 32


def draw_queries(key, part):
    key = jax.random.fold_in(key, 1)
    values = jnp.clip(2.0 * jax.random.normal(key, (SPAN, HQ * HD), jnp.float32), -8.0, 8.0)
    return values.astype(jnp.bfloat16)


def draw_suffix_kv(key, part):
    key = jax.random.fold_in(key, 2)
    values = jnp.clip(jax.random.normal(key, (2, SPAN, SLOTS * HD), jnp.float32), -4.0, 4.0)
    return values.astype(jnp.bfloat16)


def draw_hit_count(key, part):
    key = jax.random.fold_in(key, 3)
    count_key, forced_key = jax.random.split(key)
    counts = jax.random.randint(count_key, (N_CTX,), 1, HCAP + 1, jnp.int32)
    forced = jax.random.randint(forced_key, (), 0, N_CTX, jnp.int32)
    return jnp.where(jnp.arange(N_CTX, dtype=jnp.int32) == forced, HCAP, counts).astype(jnp.int32)


def draw_hit_slots(key, part):
    key = jax.random.fold_in(key, 4)
    scores = jax.random.randint(key, (N_CTX, HOLD), 0, 1 << 20, jnp.int32) * HOLD + jnp.arange(HOLD, dtype=jnp.int32)[None, :]
    ranking = jnp.argsort(scores, axis=1, stable=True)
    return ranking[:, :HCAP].astype(jnp.int32)


def levels(key, dims, cuts, smallest, high):
    loudness = 1.0
    for position, blocks in cuts:
        steps = jax.random.uniform(jax.random.fold_in(jax.random.fold_in(key, 6), position), (blocks,), jnp.float32, smallest / len(cuts), high / len(cuts))
        loudness = loudness * jnp.repeat(jnp.exp(steps), dims[position] // blocks).reshape((-1,) + (1,) * (len(dims) - 1 - position))
    return loudness


def bell_draw(rng, shape, width, reach, cuts=(), held_as=jnp.bfloat16):
    factor_of = levels(rng, shape, cuts, -0.22, 0.18) if cuts else 1.0
    drawn = jax.random.normal(rng, shape, jnp.float32) * width * factor_of
    return jnp.minimum(jnp.maximum(drawn, -reach), reach).astype(held_as)


def setup_inputs(seed: int = 0) -> dict:
    arg_keys = jax.random.split(jax.random.key(seed), 7)
    queries = draw_queries(jax.random.fold_in(arg_keys[6], 71), 0)
    suffix_kv = draw_suffix_kv(jax.random.fold_in(arg_keys[6], 71), 0)
    cache_pool = bell_draw(arg_keys[2], (2, N_CTX * HOLD, BLK, SLOTS * HD), 1.0, 6.0, ((1, 32), (3, 16)))
    hit_count = draw_hit_count(jax.random.fold_in(arg_keys[6], 71), 0)
    hit_slots = draw_hit_slots(jax.random.fold_in(arg_keys[6], 71), 0)
    out_weight = bell_draw(arg_keys[5], (HQ * HD, D), 0.2, 1.1953125, ((0, 16), (1, 32)))
    return dict(queries=queries, suffix_kv=suffix_kv, cache_pool=cache_pool, hit_count=hit_count, hit_slots=hit_slots, out_weight=out_weight)


def reference(queries, suffix_kv, cache_pool, hit_count, hit_slots, out_weight):
    holders = jnp.arange(N_CTX, dtype=jnp.int32)
    pool_index = (holders[:, None] * HOLD + hit_slots).reshape(-1).astype(jnp.int32)
    picked = jnp.take(cache_pool, pool_index, axis=1)
    prefix = picked.reshape(2, N_CTX * HCAP * BLK, SLOTS * HD)
    kept_slots = jnp.arange(HCAP, dtype=jnp.int32)[None, :] < hit_count[:, None]
    prefix_ok = jnp.repeat(kept_slots.reshape(-1), BLK)
    every_key = jnp.concatenate([prefix, suffix_kv], axis=1)
    token_pos = jnp.arange(SPAN, dtype=jnp.int32)
    visible = jnp.concatenate([jnp.broadcast_to(prefix_ok[None, :], (SPAN, prefix.shape[1])), token_pos[None, :] <= token_pos[:, None]], axis=1)
    group_size = HQ // SLOTS

    def one_head(head_index):
        slot_index = head_index // group_size
        query_rows = lax.dynamic_slice_in_dim(queries, head_index * HD, HD, 1)
        key_rows = lax.dynamic_slice_in_dim(every_key[0], slot_index * HD, HD, 1)
        value_rows = lax.dynamic_slice_in_dim(every_key[1], slot_index * HD, HD, 1)
        scores = jnp.dot(query_rows, key_rows.T, preferred_element_type=jnp.float32) / math.sqrt(HD)
        scores = jnp.where(visible, scores, -1e+30)
        row_max = lax.optimization_barrier(jnp.max(scores, axis=1, keepdims=True))
        weights = jnp.where(visible, jnp.exp(scores - row_max), 0.0)
        row_total = lax.optimization_barrier(jnp.sum(weights, axis=1, keepdims=True))
        mixed_rows = jnp.dot(weights.astype(jnp.bfloat16), value_rows, preferred_element_type=jnp.float32)
        return (mixed_rows / row_total).astype(jnp.bfloat16)
    per_head = lax.map(one_head, jnp.arange(HQ, dtype=jnp.int32))
    attention = per_head.transpose(1, 0, 2).reshape(SPAN, HQ * HD)
    return jnp.dot(attention, out_weight, preferred_element_type=jnp.float32).astype(jnp.bfloat16)
```

```python
import math

import jax
import jax.numpy as jnp
from jax import lax
from jax.experimental import pallas as pl
from jax.experimental.pallas import tpu as pltpu
from jax.sharding import PartitionSpec as P

HD = 128
HCAP = 3
BLK = 128
YH, NZ, YL, NX, CORES = 4, 8, 2, 4, 2
HEADS = 4
TOK = 128
KEYS = HCAP * BLK + TOK
HALF = TOK // CORES
WIDTH = HEADS * HD
COLS = 256
NEG = -1e30
SCALE = math.log2(math.e) / math.sqrt(HD)
Y_STEP = (0, 3, 1, 2)
Z_STEP = (0, 7, 1, 6, 2, 5, 3, 4)
MESH = pl.DeviceIdType.MESH
F32 = jnp.float32
BF16 = jnp.bfloat16


def at(yh, z, yl, x, core):
    return (yh * NZ + z, yl * (NX * CORES) + x * CORES + core)


def kernel(
    q_ref, k_ref, v_ref, w_ref, count_ref, o_ref,
    kb, vb, qb, wb, acc, mx, ob, st, rob, rst, wt, ab, cb, rb, fb, fin,
    k_ss, k_rs, q_ss, q_rs, w_ss, w_rs, s_ss, s_rs, o_ss, o_rs, t_ss, t_rs, a_ss, a_rs,
    c_ss, c_rs, f_ss, f_rs,
):
    c_index = lax.axis_index("ctx")
    t_index = lax.axis_index("tp")
    yh, z = c_index // NZ, c_index % NZ
    yl, x, core = t_index // (NX * CORES), (t_index // CORES) % NX, t_index % CORES
    chip = yl * NX + x
    other = 1 - core
    z_right, z_left = at(yh, (z + 1) % NZ, yl, x, core), at(yh, (z + NZ - 1) % NZ, yl, x, core)
    y_right, y_left = at((yh + 1) % YH, z, yl, x, core), at((yh + YH - 1) % YH, z, yl, x, core)
    sibling = at(yh, z, yl, x, other)

    def remote(src, dst, send, recv, device):
        return pltpu.make_async_remote_copy(
            src_ref=src, dst_ref=dst, send_sem=send, recv_sem=recv,
            device_id=device, device_id_type=MESH,
        )

    y_tok = yl * 2 + x // 2
    step_in = (yh + YH - y_tok) % YH
    in_yl = (y_tok // 2 + ((step_in + 1) // 2 + 1)) % 2
    in_x = ((y_tok % 2 + 1 - step_in // 2) % 2) * 2 + x % 2

    g1 = (yl + yh // 2) % 2
    g0 = (x // 2 + yh % 2) % 2
    step_out = (1 - g1) * (2 - g0) + g1 * 3 * (1 - g0)
    out_y = (yh + step_out) % YH

    def out_device(to_core):
        return at(out_y, z, yh // 2, (yh % 2) * 2 + x % 2, to_core)

    barrier = pltpu.get_barrier_semaphore()
    greeted = [z_right, z_left, sibling]
    for step in range(1, YH):
        for to_core in range(CORES):
            greeted.append(at((yh + step) % YH, z, yl, x, to_core))
    for dy in range(YL):
        for dx in range(NX):
            if (dy, dx) != (0, 0):
                greeted.append(at(yh, z, (yl + dy) % YL, (x + dx) % NX, core))
    for from_core in range(CORES):
        greeted.append(at(y_tok, z, in_yl, in_x, from_core))
    for device in greeted:
        pl.semaphore_signal(barrier, inc=1, device_id=device, device_id_type=MESH)
    pl.semaphore_wait(barrier, len(greeted))

    def kv_copy(slot, which):
        buf = (kb, vb)[which]
        if slot == 7:
            source, device = (5, z_right) if which == 0 else (6, z_left)
        else:
            source, device = max(slot - 2, 0), z_right if slot % 2 else z_left
        return remote(
            buf.at[source], buf.at[slot], k_ss.at[slot, which], k_rs.at[slot, which], device
        )

    def a_copy(slot, which):
        if slot == 7:
            source, device = (5, z_right) if which == 0 else (6, z_left)
        else:
            source, device = max(slot - 2, 0), z_right if slot % 2 else z_left
        return remote(
            ab.at[source, which], ab.at[slot, which],
            a_ss.at[slot, which], a_rs.at[slot, which], device,
        )

    def y_copy(buf, ss, rs, slot, half):
        rows = pl.ds(half * (WIDTH // 2), WIDTH // 2)
        if slot == 3:
            source, device = (1, y_right) if half == 0 else (2, y_left)
        else:
            source, device = 0, y_right if slot == 1 else y_left
        return remote(
            buf.at[source, rows], buf.at[slot, rows], ss.at[slot, half], rs.at[slot, half], device
        )

    def q_copy(slot, half):
        return y_copy(qb, q_ss, q_rs, slot, half)

    def w_copy(slot, half):
        return y_copy(wb.at[0], w_ss, w_rs, slot, half)

    def sib_copy(slot):
        return remote(wb.at[0, slot], wb.at[1, slot], s_ss.at[slot], s_rs.at[slot], sibling)

    row_minus_col = lax.broadcasted_iota(jnp.int32, (2 * TOK, TOK), 0) % TOK - (
        lax.broadcasted_iota(jnp.int32, (2 * TOK, TOK), 1)
    )

    def absorb(q_slot, step_y, slot, count, step_z):
        ones = []
        gaps = []
        for i in range(count):
            z_key = (z + step_z[i]) % NZ
            hits = count_ref[yh * NZ + z_key]
            for b in range(HCAP):
                ones.append(jnp.full((BLK, HD), jnp.where(b < hits, 1.0, 0.0), F32).astype(BF16))
            ones.append(jnp.ones((TOK, HD), BF16))
            gaps.append(((yh + step_y) % YH * NZ + z - yh * NZ - z_key) * TOK)
        ones = jnp.concatenate(ones, axis=0)
        keys = kb[slot : slot + count].reshape(count * KEYS, HD)
        values = jnp.concatenate([vb[slot : slot + count].reshape(count * KEYS, HD), ones], axis=1)

        @pl.loop(0, HEADS // 2)
        def _(pair):
            rows = pl.ds(pl.multiple_of(pair * 2 * TOK, 2 * TOK), 2 * TOK)
            scores = lax.dot_general(
                qb[q_slot, rows, :], keys, (((1,), (1,)), ((), ())), preferred_element_type=F32
            )
            parts = []
            for i in range(count):
                parts.append(scores[:, i * KEYS : i * KEYS + HCAP * BLK])
                own = scores[:, i * KEYS + HCAP * BLK : (i + 1) * KEYS]
                parts.append(jnp.where(row_minus_col + gaps[i] >= 0, own, NEG))
            scores = jnp.concatenate(parts, axis=1)
            before = mx[q_slot, rows, :]
            now = jnp.maximum(before, jnp.max(scores, axis=1, keepdims=True))
            mx[q_slot, rows, :] = now
            fade = jnp.exp2((before - now) * SCALE)
            weights = jnp.exp2((scores - now[:, :1]) * SCALE).astype(BF16)
            mixed = jnp.dot(weights, values, preferred_element_type=F32)
            acc[q_slot, rows, :] = (
                acc[q_slot, rows, :] * jnp.concatenate([fade, fade], axis=1) + mixed
            )

    kb[0] = k_ref[...]
    vb[0] = v_ref[...]
    for which in range(2):
        for slot in (1, 2):
            kv_copy(slot, which).start()
    for head in range(HEADS):
        qb[0, head * TOK : (head + 1) * TOK, :] = q_ref[:, head * HD : (head + 1) * HD]
    for slot, half in ((1, 0), (2, 1), (1, 1), (2, 0)):
        q_copy(slot, half).start()
    wb[0, 0] = w_ref[...]
    sib_copy(0).start()

    @pl.loop(0, YH)
    def _(slot):
        mx[slot] = jnp.full((WIDTH, HD), NEG, F32)
        acc[slot] = jnp.zeros((WIDTH, 2 * HD), F32)

    def pass_on(slot):
        for which in range(2):
            for s in (slot, slot + 1):
                kv_copy(s, which).wait_recv()
                if s + 2 < 7:
                    kv_copy(s + 2, which).start()
                elif (s, which) in ((5, 0), (6, 1)):
                    kv_copy(7, which).start()

    def y_step(slot):
        return (slot * 5 - slot * slot * 2) % YH if not isinstance(slot, int) else Y_STEP[slot]

    absorb(0, 0, 0, 1, Z_STEP[0:1])
    pass_on(1)
    absorb(0, 0, 1, 2, Z_STEP[1:3])
    q_copy(1, 0).wait_recv()
    q_copy(3, 0).start()
    q_copy(2, 1).wait_recv()
    q_copy(3, 1).start()
    q_copy(1, 1).wait_recv()
    q_copy(2, 0).wait_recv()
    for slot, half in ((1, 0), (2, 1), (1, 1), (2, 0)):
        w_copy(slot, half).start()
    pass_on(3)

    @pl.loop(1, 3)
    def _(slot):
        step = 3 - 2 * (slot - 1)
        absorb(slot, step, 0, 1, Z_STEP[0:1])
        absorb(slot, step, 1, 2, Z_STEP[1:3])

    @pl.loop(0, 3)
    def _(slot):
        absorb(slot, (slot * 3 + (slot // 2) * 3) % YH, 3, 2, Z_STEP[3:5])

    pass_on(5)
    q_copy(3, 0).wait_recv()
    q_copy(3, 1).wait_recv()
    absorb(3, 2, 0, 1, Z_STEP[0:1])
    absorb(3, 2, 1, 2, Z_STEP[1:3])
    absorb(3, 2, 3, 2, Z_STEP[3:5])

    @pl.loop(0, YH)
    def _(slot):
        absorb(slot, (slot * 3 + (slot // 2) * 3 + (slot // 3) * 2) % YH, 5, 2, Z_STEP[5:7])

    w_copy(1, 0).wait_recv()
    w_copy(3, 0).start()
    w_copy(2, 1).wait_recv()
    w_copy(3, 1).start()
    w_copy(1, 1).wait_recv()
    sib_copy(1).start()
    w_copy(2, 0).wait_recv()
    sib_copy(2).start()
    kv_copy(7, 0).wait_recv()
    kv_copy(7, 1).wait_recv()

    lane = lax.broadcasted_iota(jnp.int32, (TOK, HD), 1)

    def finish(slot):
        stats = jnp.ones((TOK, HD), F32)
        for head in range(HEADS):
            rows = slice(head * TOK, (head + 1) * TOK)
            total = acc[slot, rows, HD:]
            result = (acc[slot, rows, :HD] / total).astype(BF16)
            for half in range(CORES):
                ob[slot, half, :, head * HD : (head + 1) * HD] = (
                    result[half * HALF : (half + 1) * HALF]
                )
            stats = jnp.where(lane == head, mx[slot, rows, :] * SCALE, stats)
            stats = jnp.where(lane == 8 + head, total, stats)
        st[slot] = stats.T[:16, :]

    def o_copies(slot, which):
        to_core = (core, other)[which]
        device = at((yh + Y_STEP[slot]) % YH, z, yl, x, to_core)
        return (
            remote(
                st.at[slot], rst.at[which, slot], t_ss.at[slot, which], t_rs.at[slot, which], device
            ),
            remote(
                ob.at[slot, to_core], rob.at[which, slot],
                o_ss.at[slot, which], o_rs.at[slot, which], device,
            ),
        )

    for slot in (3, 1, 2, 0):
        absorb(slot, Y_STEP[slot], 7, 1, Z_STEP[7:8])
        finish(slot)
        for which in range(CORES):
            if (slot, which) != (0, 0):
                for copy in o_copies(slot, which):
                    copy.start()
    rst[0, 0] = st[0]
    rob[0, 0] = ob[0, core]
    w_copy(3, 0).wait_recv()
    w_copy(3, 1).wait_recv()
    sib_copy(3).start()
    for slot in (3, 1, 2, 0):
        for which in range(CORES):
            if (slot, which) != (0, 0):
                for copy in o_copies(slot, which):
                    copy.wait_recv()

    shares = []
    for which in range(CORES):
        top = rst[which, 0, :8]
        for slot in range(1, YH):
            top = jnp.maximum(top, rst[which, slot, :8])
        raw = [rst[which, slot, 8:] * jnp.exp2(rst[which, slot, :8] - top) for slot in range(YH)]
        whole = raw[0] + raw[1] + raw[2] + raw[3]
        shares += [share / whole for share in raw]
    wt[...] = jnp.concatenate(shares + shares, axis=0).T
    share = wt[pl.ds(pl.multiple_of(core * HALF, HALF), HALF), :]
    for which in range(CORES):
        for head in range(HEADS):
            columns = slice(head * HD, (head + 1) * HD)
            summed = jnp.zeros((HALF, HD), F32)
            for slot in range(YH):
                spot = (which * YH + slot) * 8 + head
                summed += share[:, spot : spot + 1] * rob[which, slot, :, columns].astype(F32)
            ab[0, which, :, columns] = summed.astype(BF16)
        for slot in (1, 2):
            a_copy(slot, which).start()

    def c_place(slot, w_slot):
        step = Y_STEP[w_slot]
        c1, c0 = ((1, 1), (0, 1), (0, 0), (1, 0))[step]
        z_tok = (z + Z_STEP[slot]) % NZ
        to_yl = (yh // 2 + c1) % 2
        to_x = ((yh % 2 + c0) % 2) * 2 + z_tok // 4
        return to_yl, to_x, z_tok % 4

    def c_copy(slot, w_slot):
        to_yl, to_x, spot = c_place(slot, w_slot)
        return remote(
            cb.at[slot, w_slot], rb.at[chip, spot],
            c_ss.at[slot, w_slot], c_rs.at[chip, spot], at(yh, z, to_yl, to_x, core),
        )

    def project(slot, count):
        left = [ab[slot : slot + count, which].reshape(count * HALF, WIDTH) for which in range(CORES)]
        for w_slot in (3, 1, 2, 0):
            part = jnp.dot(left[0], wb[0, w_slot], preferred_element_type=F32)
            part += jnp.dot(left[1], wb[1, w_slot], preferred_element_type=F32)
            part = part.astype(BF16)
            for i in range(count):
                cb[slot + i, w_slot] = part[i * HALF : (i + 1) * HALF]
                to_yl, to_x, spot = c_place(slot + i, w_slot)
                here = to_yl * NX + to_x == chip

                @pl.when(here)
                def _():
                    rb[chip, spot] = part[i * HALF : (i + 1) * HALF]

                @pl.when(jnp.logical_not(here))
                def _():
                    c_copy(slot + i, w_slot).start()

    for slot in range(YH):
        sib_copy(slot).wait_recv()
    project(0, 1)
    for slot in (1, 3, 5):
        for which in range(2):
            for s in (slot, slot + 1):
                a_copy(s, which).wait_recv()
                if s + 2 < 7:
                    a_copy(s + 2, which).start()
                elif (s, which) in ((5, 0), (6, 1)):
                    a_copy(7, which).start()
        project(slot, 2)
    a_copy(7, 0).wait_recv()
    a_copy(7, 1).wait_recv()
    project(7, 1)

    def f_copy(spot):
        row = (spot % 2) * TOK + core * HALF
        return remote(
            fb.at[spot], fin.at[pl.ds(pl.multiple_of(row, HALF), HALF)],
            f_ss.at[spot], f_rs.at[spot % 2, core], out_device(spot // 2),
        )

    for spot in range(4):
        @pl.loop(0, YL * NX)
        def _(source):
            @pl.when(source != chip)
            def _():
                remote(
                    cb.at[0, 0], rb.at[source, spot], c_ss.at[0, 0], c_rs.at[source, spot], sibling
                ).wait_recv()

        summed = rb[0, spot].astype(F32)
        for source in range(1, YL * NX):
            summed += rb[source, spot].astype(F32)
        fb[spot] = summed.astype(BF16)
        f_copy(spot).start()

    for spot in range(2):
        for from_core in range(CORES):
            row = spot * TOK + from_core * HALF
            remote(
                fb.at[0], fin.at[row : row + HALF], f_ss.at[0], f_rs.at[spot, from_core], sibling
            ).wait_recv()
    o_ref[...] = fin[...]

    for which in range(2):
        for slot in range(1, NZ):
            kv_copy(slot, which).wait_send()
            a_copy(slot, which).wait_send()
    for slot in range(1, YH):
        for half in range(2):
            q_copy(slot, half).wait_send()
            w_copy(slot, half).wait_send()
    for slot in range(YH):
        sib_copy(slot).wait_send()
        for which in range(CORES):
            if (slot, which) != (0, 0):
                for copy in o_copies(slot, which):
                    copy.wait_send()
    for slot in range(NZ):
        for w_slot in range(YH):
            to_yl, to_x, _ = c_place(slot, w_slot)

            @pl.when(to_yl * NX + to_x != chip)
            def _():
                c_copy(slot, w_slot).wait_send()
    for spot in range(4):
        f_copy(spot).wait_send()


def body(queries, suffix_kv, cache_pool, hit_count, hit_slots, out_weight):
    hits = hit_count[lax.axis_index("ctx")]
    slots = hit_slots[0]
    kept = jnp.arange(HCAP, dtype=jnp.int32) < hits
    key_blocks = jnp.take(cache_pool[0], jnp.where(kept, slots, slots[0]), axis=0)
    value_blocks = jnp.take(cache_pool[1], slots, axis=0)
    value_blocks = jnp.where(kept[:, None, None], value_blocks, jnp.zeros((), BF16))
    keys = jnp.concatenate([key_blocks.reshape(HCAP * BLK, HD), suffix_kv[0]], axis=0)
    values = jnp.concatenate([value_blocks.reshape(HCAP * BLK, HD), suffix_kv[1]], axis=0)
    vmem = pl.BlockSpec(memory_space=pltpu.VMEM)
    dma = pltpu.SemaphoreType.DMA
    return pl.pallas_call(
        kernel,
        out_shape=jax.ShapeDtypeStruct((2 * TOK, COLS), BF16),
        in_specs=[vmem] * 4 + [pl.BlockSpec(memory_space=pltpu.SMEM)],
        out_specs=vmem,
        scratch_shapes=[
            pltpu.VMEM((NZ, KEYS, HD), BF16),
            pltpu.VMEM((NZ, KEYS, HD), BF16),
            pltpu.VMEM((YH, WIDTH, HD), BF16),
            pltpu.VMEM((CORES, YH, WIDTH, COLS), BF16),
            pltpu.VMEM((YH, WIDTH, 2 * HD), F32),
            pltpu.VMEM((YH, WIDTH, HD), F32),
            pltpu.VMEM((YH, CORES, HALF, WIDTH), BF16),
            pltpu.VMEM((YH, 16, TOK), F32),
            pltpu.VMEM((CORES, YH, HALF, WIDTH), BF16),
            pltpu.VMEM((CORES, YH, 16, TOK), F32),
            pltpu.VMEM((TOK, HD), F32),
            pltpu.VMEM((NZ, CORES, HALF, WIDTH), BF16),
            pltpu.VMEM((NZ, YH, HALF, COLS), BF16),
            pltpu.VMEM((YL * NX, 4, HALF, COLS), BF16),
            pltpu.VMEM((4, HALF, COLS), BF16),
            pltpu.VMEM((2 * TOK, COLS), BF16),
            dma((NZ, 2)), dma((NZ, 2)),
            dma((YH, 2)), dma((YH, 2)),
            dma((YH, 2)), dma((YH, 2)),
            dma((YH,)), dma((YH,)),
            dma((YH, 2)), dma((YH, 2)),
            dma((YH, 2)), dma((YH, 2)),
            dma((NZ, 2)), dma((NZ, 2)),
            dma((NZ, YH)), dma((YL * NX, 4)),
            dma((4,)), dma((2, CORES)),
        ],
        compiler_params=pltpu.CompilerParams(
            collective_id=0, has_side_effects=True, vmem_limit_bytes=48 << 20
        ),
        cost_estimate=pl.CostEstimate(
            flops=6_000_000_000, bytes_accessed=1_000_000, transcendentals=8_400_000
        ),
        name="attention_and_projection",
    )(queries, keys, values, out_weight, hit_count)


def solution(mesh):
    placed = (
        P("ctx", "tp"),
        P(None, "ctx", "tp"),
        P(None, "ctx", None, "tp"),
        P(),
        P("ctx", None),
        P("tp", "ctx"),
    )
    return jax.shard_map(
        body, mesh=mesh, in_specs=placed, out_specs=P("tp", "ctx"), check_vma=False
    )
```

```python
import math

import jax
import jax.numpy as jnp
from jax import lax
from jax.experimental import pallas as pl
from jax.experimental.pallas import tpu as pltpu
from jax.sharding import PartitionSpec as P

HD = 128
HCAP = 3
BLK = 128
YH, NZ, YL, NX, CORES = 4, 8, 2, 4, 2
HEADS = 4
TOK = 128
KEYS = HCAP * BLK + TOK
HALF = TOK // CORES
WIDTH = HEADS * HD
COLS = 256
NEG = -1e30
SCALE = math.log2(math.e) / math.sqrt(HD)
Y_STEP = (0, 3, 1, 2)
Z_STEP = (0, 7, 1, 6, 2, 5, 3, 4)
MESH = pl.DeviceIdType.MESH
F32 = jnp.float32
BF16 = jnp.bfloat16


def at(yh, z, yl, x, core):
    return (yh * NZ + z, yl * (NX * CORES) + x * CORES + core)


def kernel(
    q_hbm, suffix_hbm, pool_hbm, w_hbm, count_ref, slots_ref, o_ref,
    q_ref, suffix_ref, pool_ref, kb, vb, qb, wb, acc, mx, ob, st, rob, rst, wt, ab, cb, rb, fb, fin,
    in_s, k_ss, k_rs, q_ss, q_rs, w_ss, w_rs, s_ss, s_rs, o_ss, o_rs, t_ss, t_rs, a_ss, a_rs,
    c_ss, c_rs, f_ss, f_rs,
):
    c_index = lax.axis_index("ctx")
    t_index = lax.axis_index("tp")
    yh, z = c_index // NZ, c_index % NZ
    yl, x, core = t_index // (NX * CORES), (t_index // CORES) % NX, t_index % CORES
    chip = yl * NX + x
    other = 1 - core
    z_right, z_left = at(yh, (z + 1) % NZ, yl, x, core), at(yh, (z + NZ - 1) % NZ, yl, x, core)
    y_right, y_left = at((yh + 1) % YH, z, yl, x, core), at((yh + YH - 1) % YH, z, yl, x, core)
    sibling = at(yh, z, yl, x, other)

    def remote(src, dst, send, recv, device):
        return pltpu.make_async_remote_copy(
            src_ref=src, dst_ref=dst, send_sem=send, recv_sem=recv,
            device_id=device, device_id_type=MESH,
        )

    y_tok = yl * 2 + x // 2
    step_in = (yh + YH - y_tok) % YH
    in_yl = (y_tok // 2 + ((step_in + 1) // 2 + 1)) % 2
    in_x = ((y_tok % 2 + 1 - step_in // 2) % 2) * 2 + x % 2

    g1 = (yl + yh // 2) % 2
    g0 = (x // 2 + yh % 2) % 2
    step_out = (1 - g1) * (2 - g0) + g1 * 3 * (1 - g0)
    out_y = (yh + step_out) % YH

    def out_device(to_core):
        return at(out_y, z, yh // 2, (yh % 2) * 2 + x % 2, to_core)

    loads = [
        pltpu.make_async_copy(pool_hbm, pool_ref, in_s.at[0]),
        pltpu.make_async_copy(suffix_hbm, suffix_ref, in_s.at[1]),
        pltpu.make_async_copy(q_hbm, q_ref, in_s.at[2]),
        pltpu.make_async_copy(w_hbm, wb.at[0, 0], in_s.at[3]),
    ]
    for load in loads:
        load.start()
    barrier = pltpu.get_barrier_semaphore()
    greeted = [z_right, z_left, sibling]
    for step in range(1, YH):
        for to_core in range(CORES):
            greeted.append(at((yh + step) % YH, z, yl, x, to_core))
    for dy in range(YL):
        for dx in range(NX):
            if (dy, dx) != (0, 0):
                greeted.append(at(yh, z, (yl + dy) % YL, (x + dx) % NX, core))
    for from_core in range(CORES):
        greeted.append(at(y_tok, z, in_yl, in_x, from_core))
    for device in greeted:
        pl.semaphore_signal(barrier, inc=1, device_id=device, device_id_type=MESH)
    pl.semaphore_wait(barrier, len(greeted))

    def kv_copy(slot, which):
        buf = (kb, vb)[which]
        if slot == 7:
            source, device = (5, z_right) if which == 0 else (6, z_left)
        else:
            source, device = max(slot - 2, 0), z_right if slot % 2 else z_left
        return remote(
            buf.at[source], buf.at[slot], k_ss.at[slot, which], k_rs.at[slot, which], device
        )

    def a_copy(slot, which):
        if slot == 7:
            source, device = (5, z_right) if which == 0 else (6, z_left)
        else:
            source, device = max(slot - 2, 0), z_right if slot % 2 else z_left
        return remote(
            ab.at[source, which], ab.at[slot, which],
            a_ss.at[slot, which], a_rs.at[slot, which], device,
        )

    def y_copy(buf, ss, rs, slot, half):
        rows = pl.ds(half * (WIDTH // 2), WIDTH // 2)
        if slot == 3:
            source, device = (1, y_right) if half == 0 else (2, y_left)
        else:
            source, device = 0, y_right if slot == 1 else y_left
        return remote(
            buf.at[source, rows], buf.at[slot, rows], ss.at[slot, half], rs.at[slot, half], device
        )

    def q_copy(slot, half):
        return y_copy(qb, q_ss, q_rs, slot, half)

    def w_copy(slot, half):
        return y_copy(wb.at[0], w_ss, w_rs, slot, half)

    def sib_copy(slot):
        return remote(wb.at[0, slot], wb.at[1, slot], s_ss.at[slot], s_rs.at[slot], sibling)

    row_minus_col = lax.broadcasted_iota(jnp.int32, (2 * TOK, TOK), 0) % TOK - (
        lax.broadcasted_iota(jnp.int32, (2 * TOK, TOK), 1)
    )

    def y_step(slot):
        if isinstance(slot, int):
            return Y_STEP[slot]
        return (slot * 3 + (slot // 2) * 3 + (slot // 3) * 2) % YH

    def absorb(q_slots, slot, count):
        ones = []
        z_keys = []
        for i in range(count):
            z_key = (z + Z_STEP[slot + i]) % NZ
            z_keys.append(z_key)
            hits = count_ref[yh * NZ + z_key]
            for b in range(HCAP):
                ones.append(jnp.full((BLK, HD), jnp.where(b < hits, 1.0, 0.0), F32).astype(BF16))
            ones.append(jnp.ones((TOK, HD), BF16))
        ones = jnp.concatenate(ones, axis=0)
        keys = kb[slot : slot + count].reshape(count * KEYS, HD)
        values = jnp.concatenate([vb[slot : slot + count].reshape(count * KEYS, HD), ones], axis=1)
        blocks = [(q_slot, pair) for q_slot in q_slots for pair in range(HEADS // 2)]
        all_scores = [
            lax.dot_general(
                qb[q_slot, pair * 2 * TOK : (pair + 1) * 2 * TOK, :], keys,
                (((1,), (1,)), ((), ())), preferred_element_type=F32,
            )
            for q_slot, pair in blocks
        ]
        for (q_slot, pair), scores in zip(blocks, all_scores):
            rows = slice(pair * 2 * TOK, (pair + 1) * 2 * TOK)
            y_query = (yh + y_step(q_slot)) % YH
            parts = []
            for i in range(count):
                gap = ((y_query - yh) * NZ + z - z_keys[i]) * TOK
                parts.append(scores[:, i * KEYS : i * KEYS + HCAP * BLK])
                own = scores[:, i * KEYS + HCAP * BLK : (i + 1) * KEYS]
                parts.append(jnp.where(row_minus_col + gap >= 0, own, NEG))
            scores = jnp.concatenate(parts, axis=1)
            before = mx[q_slot, rows, :]
            now = jnp.maximum(before, jnp.max(scores, axis=1, keepdims=True))
            mx[q_slot, rows, :] = now
            fade = jnp.exp2((before - now) * SCALE)
            weights = jnp.exp2((scores - now[:, :1]) * SCALE).astype(BF16)
            mixed = jnp.dot(weights, values, preferred_element_type=F32)
            acc[q_slot, rows, :] = (
                acc[q_slot, rows, :] * jnp.concatenate([fade, fade], axis=1) + mixed
            )

    loads[0].wait()
    loads[1].wait()
    hits = count_ref[c_index]
    for b in range(HCAP):
        rows = slice(b * BLK, (b + 1) * BLK)
        kept = b < hits
        kb[0, rows, :] = pool_ref[0, jnp.where(kept, slots_ref[0, b], slots_ref[0, 0])]
        keep = jnp.full((BLK, HD), jnp.where(kept, 1.0, 0.0), F32).astype(BF16)
        vb[0, rows, :] = pool_ref[1, slots_ref[0, b]] * keep
    kb[0, HCAP * BLK :, :] = suffix_ref[0]
    vb[0, HCAP * BLK :, :] = suffix_ref[1]
    for which in range(2):
        for slot in (1, 2):
            kv_copy(slot, which).start()
    loads[2].wait()
    for head in range(HEADS):
        qb[0, head * TOK : (head + 1) * TOK, :] = q_ref[:, head * HD : (head + 1) * HD]
    for slot, half in ((1, 0), (2, 1), (1, 1), (2, 0)):
        q_copy(slot, half).start()
    loads[3].wait()
    sib_copy(0).start()

    @pl.loop(0, YH)
    def _(slot):
        mx[slot] = jnp.full((WIDTH, HD), NEG, F32)
        acc[slot] = jnp.zeros((WIDTH, 2 * HD), F32)

    def pass_on(slot):
        for which in range(2):
            for s in (slot, slot + 1):
                kv_copy(s, which).wait_recv()
                if s + 2 < 7:
                    kv_copy(s + 2, which).start()
                elif (s, which) in ((5, 0), (6, 1)):
                    kv_copy(7, which).start()

    absorb([0], 0, 1)
    pass_on(1)
    absorb([0], 1, 2)
    q_copy(1, 0).wait_recv()
    q_copy(3, 0).start()
    q_copy(2, 1).wait_recv()
    q_copy(3, 1).start()
    q_copy(1, 1).wait_recv()
    q_copy(2, 0).wait_recv()
    for slot, half in ((1, 0), (2, 1), (1, 1), (2, 0)):
        w_copy(slot, half).start()
    pass_on(3)

    absorb([1, 2], 0, 3)

    @pl.loop(0, 3)
    def _(slot):
        absorb([slot], 3, 2)

    pass_on(5)
    q_copy(3, 0).wait_recv()
    q_copy(3, 1).wait_recv()
    absorb([3], 0, 5)

    @pl.loop(0, 2)
    def _(pair):
        absorb([2 * pair, 2 * pair + 1], 5, 2)

    w_copy(1, 0).wait_recv()
    w_copy(3, 0).start()
    w_copy(2, 1).wait_recv()
    w_copy(3, 1).start()
    w_copy(1, 1).wait_recv()
    sib_copy(1).start()
    w_copy(2, 0).wait_recv()
    sib_copy(2).start()
    kv_copy(7, 0).wait_recv()
    kv_copy(7, 1).wait_recv()

    lane = lax.broadcasted_iota(jnp.int32, (TOK, HD), 1)

    def finish(slot):
        stats = jnp.ones((TOK, HD), F32)
        for head in range(HEADS):
            rows = slice(head * TOK, (head + 1) * TOK)
            total = acc[slot, rows, HD:]
            result = (acc[slot, rows, :HD] / total).astype(BF16)
            for half in range(CORES):
                ob[slot, half, :, head * HD : (head + 1) * HD] = (
                    result[half * HALF : (half + 1) * HALF]
                )
            stats = jnp.where(lane == head, mx[slot, rows, :] * SCALE, stats)
            stats = jnp.where(lane == 8 + head, total, stats)
        st[slot] = stats.T[:16, :]

    def o_copies(slot, which):
        to_core = (core, other)[which]
        device = at((yh + Y_STEP[slot]) % YH, z, yl, x, to_core)
        return (
            remote(
                st.at[slot], rst.at[which, slot], t_ss.at[slot, which], t_rs.at[slot, which], device
            ),
            remote(
                ob.at[slot, to_core], rob.at[which, slot],
                o_ss.at[slot, which], o_rs.at[slot, which], device,
            ),
        )

    for pair in ((3, 1), (2, 0)):
        absorb(pair, 7, 1)
        for slot in pair:
            finish(slot)
            for which in range(CORES):
                if (slot, which) != (0, 0):
                    for copy in o_copies(slot, which):
                        copy.start()
    rst[0, 0] = st[0]
    rob[0, 0] = ob[0, core]
    w_copy(3, 0).wait_recv()
    w_copy(3, 1).wait_recv()
    sib_copy(3).start()
    for slot in (3, 1, 2, 0):
        for which in range(CORES):
            if (slot, which) != (0, 0):
                for copy in o_copies(slot, which):
                    copy.wait_recv()

    shares = []
    for which in range(CORES):
        top = rst[which, 0, :8]
        for slot in range(1, YH):
            top = jnp.maximum(top, rst[which, slot, :8])
        raw = [rst[which, slot, 8:] * jnp.exp2(rst[which, slot, :8] - top) for slot in range(YH)]
        whole = raw[0] + raw[1] + raw[2] + raw[3]
        shares += [share / whole for share in raw]
    wt[...] = jnp.concatenate(shares + shares, axis=0).T
    share = wt[pl.ds(pl.multiple_of(core * HALF, HALF), HALF), :]
    for which in range(CORES):
        for head in range(HEADS):
            columns = slice(head * HD, (head + 1) * HD)
            summed = jnp.zeros((HALF, HD), F32)
            for slot in range(YH):
                spot = (which * YH + slot) * 8 + head
                summed += share[:, spot : spot + 1] * rob[which, slot, :, columns].astype(F32)
            ab[0, which, :, columns] = summed.astype(BF16)
        for slot in (1, 2):
            a_copy(slot, which).start()

    def c_place(slot, w_slot):
        step = Y_STEP[w_slot]
        c1, c0 = ((1, 1), (0, 1), (0, 0), (1, 0))[step]
        z_tok = (z + Z_STEP[slot]) % NZ
        to_yl = (yh // 2 + c1) % 2
        to_x = ((yh % 2 + c0) % 2) * 2 + z_tok // 4
        return to_yl, to_x, z_tok % 4

    def c_copy(slot, w_slot):
        to_yl, to_x, spot = c_place(slot, w_slot)
        return remote(
            cb.at[slot, w_slot], rb.at[chip, spot],
            c_ss.at[slot, w_slot], c_rs.at[chip, spot], at(yh, z, to_yl, to_x, core),
        )

    def project(slot, count):
        left = [ab[slot : slot + count, which].reshape(count * HALF, WIDTH) for which in range(CORES)]
        for w_slot in (3, 1, 2, 0):
            part = jnp.dot(left[0], wb[0, w_slot], preferred_element_type=F32)
            part += jnp.dot(left[1], wb[1, w_slot], preferred_element_type=F32)
            part = part.astype(BF16)
            for i in range(count):
                cb[slot + i, w_slot] = part[i * HALF : (i + 1) * HALF]
                to_yl, to_x, spot = c_place(slot + i, w_slot)
                here = to_yl * NX + to_x == chip

                @pl.when(here)
                def _():
                    rb[chip, spot] = part[i * HALF : (i + 1) * HALF]

                @pl.when(jnp.logical_not(here))
                def _():
                    c_copy(slot + i, w_slot).start()

    for slot in range(YH):
        sib_copy(slot).wait_recv()
    project(0, 1)
    for slot in (1, 3, 5):
        for which in range(2):
            for s in (slot, slot + 1):
                a_copy(s, which).wait_recv()
                if s + 2 < 7:
                    a_copy(s + 2, which).start()
                elif (s, which) in ((5, 0), (6, 1)):
                    a_copy(7, which).start()
        project(slot, 2)
    a_copy(7, 0).wait_recv()
    a_copy(7, 1).wait_recv()
    project(7, 1)

    def f_copy(spot):
        row = (spot % 2) * TOK + core * HALF
        return remote(
            fb.at[spot], fin.at[pl.ds(pl.multiple_of(row, HALF), HALF)],
            f_ss.at[spot], f_rs.at[spot % 2, core], out_device(spot // 2),
        )

    for spot in range(4):
        @pl.loop(0, YL * NX)
        def _(source):
            @pl.when(source != chip)
            def _():
                remote(
                    cb.at[0, 0], rb.at[source, spot], c_ss.at[0, 0], c_rs.at[source, spot], sibling
                ).wait_recv()

        summed = rb[0, spot].astype(F32)
        for source in range(1, YL * NX):
            summed += rb[source, spot].astype(F32)
        fb[spot] = summed.astype(BF16)
        f_copy(spot).start()

    for spot in range(2):
        for from_core in range(CORES):
            row = spot * TOK + from_core * HALF
            remote(
                fb.at[0], fin.at[row : row + HALF], f_ss.at[0], f_rs.at[spot, from_core], sibling
            ).wait_recv()
    o_ref[...] = fin[...]

    for which in range(2):
        for slot in range(1, NZ):
            kv_copy(slot, which).wait_send()
            a_copy(slot, which).wait_send()
    for slot in range(1, YH):
        for half in range(2):
            q_copy(slot, half).wait_send()
            w_copy(slot, half).wait_send()
    for slot in range(YH):
        sib_copy(slot).wait_send()
        for which in range(CORES):
            if (slot, which) != (0, 0):
                for copy in o_copies(slot, which):
                    copy.wait_send()
    for slot in range(NZ):
        for w_slot in range(YH):
            to_yl, to_x, _ = c_place(slot, w_slot)

            @pl.when(to_yl * NX + to_x != chip)
            def _():
                c_copy(slot, w_slot).wait_send()
    for spot in range(4):
        f_copy(spot).wait_send()


def body(queries, suffix_kv, cache_pool, hit_count, hit_slots, out_weight):
    vmem = pl.BlockSpec(memory_space=pltpu.VMEM)
    hbm = pl.BlockSpec(memory_space=pl.ANY)
    smem = pl.BlockSpec(memory_space=pltpu.SMEM)
    dma = pltpu.SemaphoreType.DMA
    return pl.pallas_call(
        kernel,
        out_shape=jax.ShapeDtypeStruct((2 * TOK, COLS), BF16),
        in_specs=[hbm] * 4 + [smem] * 2,
        out_specs=vmem,
        scratch_shapes=[
            pltpu.VMEM(queries.shape, BF16),
            pltpu.VMEM(suffix_kv.shape, BF16),
            pltpu.VMEM(cache_pool.shape, BF16),
            pltpu.VMEM((NZ, KEYS, HD), BF16),
            pltpu.VMEM((NZ, KEYS, HD), BF16),
            pltpu.VMEM((YH, WIDTH, HD), BF16),
            pltpu.VMEM((CORES, YH, WIDTH, COLS), BF16),
            pltpu.VMEM((YH, WIDTH, 2 * HD), F32),
            pltpu.VMEM((YH, WIDTH, HD), F32),
            pltpu.VMEM((YH, CORES, HALF, WIDTH), BF16),
            pltpu.VMEM((YH, 16, TOK), F32),
            pltpu.VMEM((CORES, YH, HALF, WIDTH), BF16),
            pltpu.VMEM((CORES, YH, 16, TOK), F32),
            pltpu.VMEM((TOK, HD), F32),
            pltpu.VMEM((NZ, CORES, HALF, WIDTH), BF16),
            pltpu.VMEM((NZ, YH, HALF, COLS), BF16),
            pltpu.VMEM((YL * NX, 4, HALF, COLS), BF16),
            pltpu.VMEM((4, HALF, COLS), BF16),
            pltpu.VMEM((2 * TOK, COLS), BF16),
            dma((4,)),
            dma((NZ, 2)), dma((NZ, 2)),
            dma((YH, 2)), dma((YH, 2)),
            dma((YH, 2)), dma((YH, 2)),
            dma((YH,)), dma((YH,)),
            dma((YH, 2)), dma((YH, 2)),
            dma((YH, 2)), dma((YH, 2)),
            dma((NZ, 2)), dma((NZ, 2)),
            dma((NZ, YH)), dma((YL * NX, 4)),
            dma((4,)), dma((2, CORES)),
        ],
        compiler_params=pltpu.CompilerParams(
            collective_id=0, has_side_effects=True, vmem_limit_bytes=62 << 20
        ),
        cost_estimate=pl.CostEstimate(
            flops=6_000_000_000, bytes_accessed=1_000_000, transcendentals=8_400_000
        ),
        name="attention_and_projection",
    )(queries, suffix_kv, cache_pool, out_weight, hit_count, hit_slots)


def solution(mesh):
    placed = (
        P("ctx", "tp"),
        P(None, "ctx", "tp"),
        P(None, "ctx", None, "tp"),
        P(),
        P("ctx", None),
        P("tp", "ctx"),
    )
    return jax.shard_map(
        body, mesh=mesh, in_specs=placed, out_specs=P("tp", "ctx"), check_vma=False
    )
```

```python
import math

import jax
import jax.numpy as jnp
from jax import lax
from jax.experimental import pallas as pl
from jax.experimental.pallas import tpu as pltpu
from jax.sharding import PartitionSpec as P

HD = 128
HCAP = 3
BLK = 128
YH, NZ, YL, NX, CORES = 4, 8, 2, 4, 2
HEADS = 4
TOK = 128
KEYS = HCAP * BLK + TOK
HALF = TOK // CORES
GROUPS = 4
PART = HALF // GROUPS
WIDTH = HEADS * HD
COLS = 256
NEG = -1e30
SCALE = math.log2(math.e) / math.sqrt(HD)
Y_STEP = (0, 3, 1, 2)
Z_STEP = (0, 7, 1, 6, 2, 5, 3, 4)
MESH = pl.DeviceIdType.MESH
F32 = jnp.float32
BF16 = jnp.bfloat16


def at(yh, z, yl, x, core):
    return (yh * NZ + z, yl * (NX * CORES) + x * CORES + core)


def kernel(
    q_hbm, suffix_hbm, pool_hbm, w_hbm, count_ref, slots_ref, o_ref,
    q_ref, suffix_ref, pool_ref, kb, vb, qb, wb, acc, mx, ob, st, rob, rst, wt, ab, cb, rb, fb, fin,
    in_s, k_ss, k_rs, q_ss, q_rs, w_ss, w_rs, s_ss, s_rs, o_ss, o_rs, t_ss, t_rs, a_ss, a_rs,
    c_ss, c_rs, f_ss, f_rs,
):
    c_index = lax.axis_index("ctx")
    t_index = lax.axis_index("tp")
    yh, z = c_index // NZ, c_index % NZ
    yl, x, core = t_index // (NX * CORES), (t_index // CORES) % NX, t_index % CORES
    chip = yl * NX + x
    other = 1 - core
    z_right, z_left = at(yh, (z + 1) % NZ, yl, x, core), at(yh, (z + NZ - 1) % NZ, yl, x, core)
    y_right, y_left = at((yh + 1) % YH, z, yl, x, core), at((yh + YH - 1) % YH, z, yl, x, core)
    sibling = at(yh, z, yl, x, other)

    def remote(src, dst, send, recv, device):
        return pltpu.make_async_remote_copy(
            src_ref=src, dst_ref=dst, send_sem=send, recv_sem=recv,
            device_id=device, device_id_type=MESH,
        )

    y_tok = yl * 2 + x // 2
    step_in = (yh + YH - y_tok) % YH
    in_yl = (y_tok // 2 + ((step_in + 1) // 2 + 1)) % 2
    in_x = ((y_tok % 2 + 1 - step_in // 2) % 2) * 2 + x % 2

    g1 = (yl + yh // 2) % 2
    g0 = (x // 2 + yh % 2) % 2
    step_out = (1 - g1) * (2 - g0) + g1 * 3 * (1 - g0)
    out_y = (yh + step_out) % YH

    def out_device(to_core):
        return at(out_y, z, yh // 2, (yh % 2) * 2 + x % 2, to_core)

    barrier = pltpu.get_barrier_semaphore()
    greeted = [z_right, z_left, sibling]
    for step in range(1, YH):
        for to_core in range(CORES):
            greeted.append(at((yh + step) % YH, z, yl, x, to_core))
    for dy in range(YL):
        for dx in range(NX):
            if (dy, dx) != (0, 0):
                greeted.append(at(yh, z, (yl + dy) % YL, (x + dx) % NX, core))
    for from_core in range(CORES):
        greeted.append(at(y_tok, z, in_yl, in_x, from_core))
    for device in greeted:
        pl.semaphore_signal(barrier, inc=1, device_id=device, device_id_type=MESH)
    loads = [
        pltpu.make_async_copy(pool_hbm, pool_ref, in_s.at[0]),
        pltpu.make_async_copy(suffix_hbm, suffix_ref, in_s.at[1]),
        pltpu.make_async_copy(q_hbm, q_ref, in_s.at[2]),
        pltpu.make_async_copy(w_hbm, wb.at[0, 0], in_s.at[3]),
    ]
    for load in loads:
        load.start()

    def kv_copy(slot, which, part):
        buf = (kb, vb)[which]
        rows = pl.ds(part * (KEYS // 2), KEYS // 2)
        if slot == 7:
            source, device = (5, z_right) if which == 0 else (6, z_left)
        else:
            source, device = max(slot - 2, 0), z_right if slot % 2 else z_left
        return remote(
            buf.at[source, rows], buf.at[slot, rows],
            k_ss.at[slot, which, part], k_rs.at[slot, which, part], device,
        )

    def a_copy(slot, group, which):
        if slot == 7:
            source, device = (5, z_right) if which == 0 else (6, z_left)
            src, dst = ab.at[source, group, which], ab.at[slot, group, which]
        else:
            source, device = max(slot - 2, 0), z_right if slot % 2 else z_left
            src, dst = ab.at[source, group], ab.at[slot, group]
        return remote(
            src, dst, a_ss.at[slot, group, which], a_rs.at[slot, group, which], device
        )

    def y_copy(buf, ss, rs, slot, half):
        rows = pl.ds(half * (WIDTH // 2), WIDTH // 2)
        if slot == 3:
            source, device = (1, y_right) if half == 0 else (2, y_left)
        else:
            source, device = 0, y_right if slot == 1 else y_left
        return remote(
            buf.at[source, rows], buf.at[slot, rows], ss.at[slot, half], rs.at[slot, half], device
        )

    def q_copy(slot, half):
        return y_copy(qb, q_ss, q_rs, slot, half)

    def w_copy(slot, half):
        return y_copy(wb.at[0], w_ss, w_rs, slot, half)

    def sib_copy(slot):
        return remote(wb.at[0, slot], wb.at[1, slot], s_ss.at[slot], s_rs.at[slot], sibling)

    row_minus_col = lax.broadcasted_iota(jnp.int32, (2 * TOK, TOK), 0) % TOK - (
        lax.broadcasted_iota(jnp.int32, (2 * TOK, TOK), 1)
    )

    def y_step(slot):
        if isinstance(slot, int):
            return Y_STEP[slot]
        return (slot * 3 + (slot // 2) * 3 + (slot // 3) * 2) % YH

    def absorb(q_slots, slot, count):
        ones = []
        z_keys = []
        for i in range(count):
            z_key = (z + Z_STEP[slot + i]) % NZ
            z_keys.append(z_key)
            hits = count_ref[yh * NZ + z_key]
            for b in range(HCAP):
                ones.append(jnp.full((BLK, HD), jnp.where(b < hits, 1.0, 0.0), F32).astype(BF16))
            ones.append(jnp.ones((TOK, HD), BF16))
        ones = jnp.concatenate(ones, axis=0)
        keys = kb[slot : slot + count].reshape(count * KEYS, HD)
        values = jnp.concatenate([vb[slot : slot + count].reshape(count * KEYS, HD), ones], axis=1)
        blocks = [(q_slot, pair) for q_slot in q_slots for pair in range(HEADS // 2)]
        all_scores = [
            lax.dot_general(
                qb[q_slot, pair * 2 * TOK : (pair + 1) * 2 * TOK, :], keys,
                (((1,), (1,)), ((), ())), preferred_element_type=F32,
            )
            for q_slot, pair in blocks
        ]
        for (q_slot, pair), scores in zip(blocks, all_scores):
            rows = slice(pair * 2 * TOK, (pair + 1) * 2 * TOK)
            y_query = (yh + y_step(q_slot)) % YH
            parts = []
            for i in range(count):
                gap = ((y_query - yh) * NZ + z - z_keys[i]) * TOK
                parts.append(scores[:, i * KEYS : i * KEYS + HCAP * BLK])
                own = scores[:, i * KEYS + HCAP * BLK : (i + 1) * KEYS]
                parts.append(jnp.where(row_minus_col + gap >= 0, own, NEG))
            scores = jnp.concatenate(parts, axis=1)
            before = mx[q_slot, rows, :]
            now = jnp.maximum(before, jnp.max(scores, axis=1, keepdims=True))
            mx[q_slot, rows, :] = now
            fade = jnp.exp2((before - now) * SCALE)
            weights = jnp.exp2((scores - now[:, :1]) * SCALE).astype(BF16)
            mixed = jnp.dot(weights, values, preferred_element_type=F32)
            acc[q_slot, rows, :] = (
                acc[q_slot, rows, :] * jnp.concatenate([fade, fade], axis=1) + mixed
            )

    loads[0].wait()
    loads[1].wait()
    hits = count_ref[c_index]
    for b in range(HCAP):
        rows = slice(b * BLK, (b + 1) * BLK)
        kept = b < hits
        kb[0, rows, :] = pool_ref[0, jnp.where(kept, slots_ref[0, b], slots_ref[0, 0])]
        keep = jnp.full((BLK, HD), jnp.where(kept, 1.0, 0.0), F32).astype(BF16)
        vb[0, rows, :] = pool_ref[1, slots_ref[0, b]] * keep
    kb[0, HCAP * BLK :, :] = suffix_ref[0]
    vb[0, HCAP * BLK :, :] = suffix_ref[1]
    loads[2].wait()
    for head in range(HEADS):
        qb[0, head * TOK : (head + 1) * TOK, :] = q_ref[:, head * HD : (head + 1) * HD]
    pl.semaphore_wait(barrier, len(greeted))
    for which in range(2):
        for part in range(2):
            for slot in (1, 2):
                kv_copy(slot, which, part).start()
    for slot, half in ((1, 0), (2, 1), (1, 1), (2, 0)):
        q_copy(slot, half).start()
    loads[3].wait()
    sib_copy(0).start()

    @pl.loop(0, YH)
    def _(slot):
        mx[slot] = jnp.full((WIDTH, HD), NEG, F32)
        acc[slot] = jnp.zeros((WIDTH, 2 * HD), F32)

    def pass_on(slot):
        for which in range(2):
            for part in range(2):
                for s in (slot, slot + 1):
                    kv_copy(s, which, part).wait_recv()
                    if s + 2 < 7:
                        kv_copy(s + 2, which, part).start()
                    elif (s, which) in ((5, 0), (6, 1)):
                        kv_copy(7, which, part).start()

    absorb([0], 0, 1)
    pass_on(1)
    absorb([0], 1, 2)
    q_copy(1, 0).wait_recv()
    q_copy(3, 0).start()
    q_copy(2, 1).wait_recv()
    q_copy(3, 1).start()
    q_copy(1, 1).wait_recv()
    q_copy(2, 0).wait_recv()
    for slot, half in ((1, 0), (2, 1), (1, 1), (2, 0)):
        w_copy(slot, half).start()
    pass_on(3)

    absorb([1, 2], 0, 3)

    @pl.loop(0, 3)
    def _(slot):
        absorb([slot], 3, 2)

    pass_on(5)
    q_copy(3, 0).wait_recv()
    q_copy(3, 1).wait_recv()
    absorb([3], 0, 5)

    @pl.loop(0, 2)
    def _(pair):
        absorb([2 * pair, 2 * pair + 1], 5, 2)

    w_copy(1, 0).wait_recv()
    w_copy(3, 0).start()
    w_copy(2, 1).wait_recv()
    w_copy(3, 1).start()
    w_copy(1, 1).wait_recv()
    sib_copy(1).start()
    w_copy(2, 0).wait_recv()
    sib_copy(2).start()
    for which in range(2):
        for part in range(2):
            kv_copy(7, which, part).wait_recv()

    lane = lax.broadcasted_iota(jnp.int32, (TOK, HD), 1)

    def finish(slot):
        stats = jnp.ones((TOK, HD), F32)
        for head in range(HEADS):
            rows = slice(head * TOK, (head + 1) * TOK)
            total = acc[slot, rows, HD:]
            result = (acc[slot, rows, :HD] / total).astype(BF16)
            for to_core in range(CORES):
                for group in range(GROUPS):
                    row = to_core * HALF + group * PART
                    ob[slot, to_core, group, :, head * HD : (head + 1) * HD] = (
                        result[row : row + PART]
                    )
            stats = jnp.where(lane == head, mx[slot, rows, :] * SCALE, stats)
            stats = jnp.where(lane == 8 + head, total, stats)
        st[slot] = stats.T[:16, :]

    def o_copies(slot, which, group):
        to_core = (core, other)[which]
        device = at((yh + Y_STEP[slot]) % YH, z, yl, x, to_core)
        copies = []
        if group == 0:
            copies.append(
                remote(
                    st.at[slot], rst.at[which, slot],
                    t_ss.at[slot, which], t_rs.at[slot, which], device,
                )
            )
        copies.append(
            remote(
                ob.at[slot, to_core, group], rob.at[which, slot, group],
                o_ss.at[slot, which, group], o_rs.at[slot, which, group], device,
            )
        )
        return copies

    def all_o_copies(slots, group):
        return [
            copy
            for slot in slots
            for which in range(CORES)
            if (slot, which) != (0, 0)
            for copy in o_copies(slot, which, group)
        ]

    for pair in ((3, 1), (2, 0)):
        absorb(pair, 7, 1)
        for slot in pair:
            finish(slot)
            for copy in all_o_copies([slot], 0):
                copy.start()
    for group in range(1, GROUPS):
        for copy in all_o_copies((3, 1, 2, 0), group):
            copy.start()
    rst[0, 0] = st[0]
    rob[0, 0] = ob[0, core]
    w_copy(3, 0).wait_recv()
    w_copy(3, 1).wait_recv()
    sib_copy(3).start()

    for group in range(GROUPS):
        for copy in all_o_copies((3, 1, 2, 0), group):
            copy.wait_recv()
        if group == 0:
            shares = []
            for which in range(CORES):
                top = rst[which, 0, :8]
                for slot in range(1, YH):
                    top = jnp.maximum(top, rst[which, slot, :8])
                raw = [
                    rst[which, slot, 8:] * jnp.exp2(rst[which, slot, :8] - top)
                    for slot in range(YH)
                ]
                whole = raw[0] + raw[1] + raw[2] + raw[3]
                shares += [share / whole for share in raw]
            wt[...] = jnp.concatenate(shares + shares, axis=0).T
        share = wt[pl.ds(pl.multiple_of(core * HALF + group * PART, PART), PART), :]
        for which in range(CORES):
            for head in range(HEADS):
                columns = slice(head * HD, (head + 1) * HD)
                summed = jnp.zeros((PART, HD), F32)
                for slot in range(YH):
                    spot = (which * YH + slot) * 8 + head
                    summed += (
                        share[:, spot : spot + 1] * rob[which, slot, group, :, columns].astype(F32)
                    )
                ab[0, group, which, :, columns] = summed.astype(BF16)
        for slot in (1, 2):
            a_copy(slot, group, 0).start()

    def c_place(slot, w_slot):
        step = Y_STEP[w_slot]
        c1, c0 = ((1, 1), (0, 1), (0, 0), (1, 0))[step]
        z_tok = (z + Z_STEP[slot]) % NZ
        to_yl = (yh // 2 + c1) % 2
        to_x = ((yh % 2 + c0) % 2) * 2 + z_tok // 4
        return to_yl, to_x, z_tok % 4

    def c_copy(slot, w_slot):
        to_yl, to_x, spot = c_place(slot, w_slot)
        return remote(
            cb.at[slot, w_slot], rb.at[chip, spot],
            c_ss.at[slot, w_slot], c_rs.at[chip, spot], at(yh, z, to_yl, to_x, core),
        )

    def project(slot, count):
        left = [
            ab[slot : slot + count, :, which].reshape(count * HALF, WIDTH)
            for which in range(CORES)
        ]
        for w_slot in (3, 1, 2, 0):
            part = jnp.dot(left[0], wb[0, w_slot], preferred_element_type=F32)
            part += jnp.dot(left[1], wb[1, w_slot], preferred_element_type=F32)
            part = part.astype(BF16)
            for i in range(count):
                cb[slot + i, w_slot] = part[i * HALF : (i + 1) * HALF]
                to_yl, to_x, spot = c_place(slot + i, w_slot)
                here = to_yl * NX + to_x == chip

                @pl.when(here)
                def _():
                    rb[chip, spot] = part[i * HALF : (i + 1) * HALF]

                @pl.when(jnp.logical_not(here))
                def _():
                    c_copy(slot + i, w_slot).start()

    def pass_a(slot, group):
        for s in (slot, slot + 1):
            a_copy(s, group, 0).wait_recv()
            if s + 2 < 7:
                a_copy(s + 2, group, 0).start()
            else:
                a_copy(7, group, s - 5).start()

    def f_copy(spot):
        row = (spot % 2) * TOK + core * HALF
        return remote(
            fb.at[spot], fin.at[pl.ds(pl.multiple_of(row, HALF), HALF)],
            f_ss.at[spot], f_rs.at[spot % 2, core], out_device(spot // 2),
        )

    def reduce(slot):
        z_tok = (z + Z_STEP[slot]) % NZ
        spot = z_tok % 4

        @pl.when(z_tok // 4 == x % 2)
        def _():
            @pl.loop(0, YL * NX)
            def _(source):
                @pl.when(source != chip)
                def _():
                    remote(
                        cb.at[0, 0], rb.at[source, spot],
                        c_ss.at[0, 0], c_rs.at[source, spot], sibling,
                    ).wait_recv()

            summed = rb[0, spot].astype(F32)
            for source in range(1, YL * NX):
                summed += rb[source, spot].astype(F32)
            fb[spot] = summed.astype(BF16)
            f_copy(spot).start()

    for slot in range(YH):
        sib_copy(slot).wait_recv()
    pass_a(1, 0)
    project(0, 1)
    for group in range(1, GROUPS):
        pass_a(1, group)
    pass_a(3, 0)
    project(1, 2)
    for group in range(1, GROUPS):
        pass_a(3, group)
    pass_a(5, 0)
    project(3, 2)
    for group in range(1, GROUPS):
        pass_a(5, group)
    reduce(0)
    project(5, 2)
    reduce(1)
    reduce(2)
    for group in range(GROUPS):
        for which in range(2):
            a_copy(7, group, which).wait_recv()
    project(7, 1)
    for slot in range(3, NZ):
        reduce(slot)

    for spot in range(2):
        for from_core in range(CORES):
            row = spot * TOK + from_core * HALF
            remote(
                fb.at[0], fin.at[row : row + HALF], f_ss.at[0], f_rs.at[spot, from_core], sibling
            ).wait_recv()
    o_ref[...] = fin[...]

    for which in range(2):
        for slot in range(1, NZ):
            for part in range(2):
                kv_copy(slot, which, part).wait_send()
    for group in range(GROUPS):
        for slot in range(1, NZ - 1):
            a_copy(slot, group, 0).wait_send()
        for which in range(2):
            a_copy(NZ - 1, group, which).wait_send()
        for copy in all_o_copies(range(YH), group):
            copy.wait_send()
    for slot in range(1, YH):
        for half in range(2):
            q_copy(slot, half).wait_send()
            w_copy(slot, half).wait_send()
    for slot in range(YH):
        sib_copy(slot).wait_send()
    for slot in range(NZ):
        for w_slot in range(YH):
            to_yl, to_x, _ = c_place(slot, w_slot)

            @pl.when(to_yl * NX + to_x != chip)
            def _():
                c_copy(slot, w_slot).wait_send()
    for spot in range(4):
        f_copy(spot).wait_send()


def body(queries, suffix_kv, cache_pool, hit_count, hit_slots, out_weight):
    vmem = pl.BlockSpec(memory_space=pltpu.VMEM)
    hbm = pl.BlockSpec(memory_space=pl.ANY)
    smem = pl.BlockSpec(memory_space=pltpu.SMEM)
    dma = pltpu.SemaphoreType.DMA
    return pl.pallas_call(
        kernel,
        out_shape=jax.ShapeDtypeStruct((2 * TOK, COLS), BF16),
        in_specs=[hbm] * 4 + [smem] * 2,
        out_specs=vmem,
        scratch_shapes=[
            pltpu.VMEM(queries.shape, BF16),
            pltpu.VMEM(suffix_kv.shape, BF16),
            pltpu.VMEM(cache_pool.shape, BF16),
            pltpu.VMEM((NZ, KEYS, HD), BF16),
            pltpu.VMEM((NZ, KEYS, HD), BF16),
            pltpu.VMEM((YH, WIDTH, HD), BF16),
            pltpu.VMEM((CORES, YH, WIDTH, COLS), BF16),
            pltpu.VMEM((YH, WIDTH, 2 * HD), F32),
            pltpu.VMEM((YH, WIDTH, HD), F32),
            pltpu.VMEM((YH, CORES, GROUPS, PART, WIDTH), BF16),
            pltpu.VMEM((YH, 16, TOK), F32),
            pltpu.VMEM((CORES, YH, GROUPS, PART, WIDTH), BF16),
            pltpu.VMEM((CORES, YH, 16, TOK), F32),
            pltpu.VMEM((TOK, HD), F32),
            pltpu.VMEM((NZ, GROUPS, CORES, PART, WIDTH), BF16),
            pltpu.VMEM((NZ, YH, HALF, COLS), BF16),
            pltpu.VMEM((YL * NX, 4, HALF, COLS), BF16),
            pltpu.VMEM((4, HALF, COLS), BF16),
            pltpu.VMEM((2 * TOK, COLS), BF16),
            dma((4,)),
            dma((NZ, 2, 2)), dma((NZ, 2, 2)),
            dma((YH, 2)), dma((YH, 2)),
            dma((YH, 2)), dma((YH, 2)),
            dma((YH,)), dma((YH,)),
            dma((YH, 2, GROUPS)), dma((YH, 2, GROUPS)),
            dma((YH, 2)), dma((YH, 2)),
            dma((NZ, GROUPS, 2)), dma((NZ, GROUPS, 2)),
            dma((NZ, YH)), dma((YL * NX, 4)),
            dma((4,)), dma((2, CORES)),
        ],
        compiler_params=pltpu.CompilerParams(
            collective_id=0, has_side_effects=True, vmem_limit_bytes=62 << 20
        ),
        cost_estimate=pl.CostEstimate(
            flops=6_000_000_000, bytes_accessed=1_000_000, transcendentals=8_400_000
        ),
        name="attention_and_projection",
    )(queries, suffix_kv, cache_pool, out_weight, hit_count, hit_slots)


def solution(mesh):
    placed = (
        P("ctx", "tp"),
        P(None, "ctx", "tp"),
        P(None, "ctx", None, "tp"),
        P(),
        P("ctx", None),
        P("tp", "ctx"),
    )
    return jax.shard_map(
        body, mesh=mesh, in_specs=placed, out_specs=P("tp", "ctx"), check_vma=False
    )
```

```python
import math

import jax
import jax.numpy as jnp
from jax import lax
from jax.experimental import pallas as pl
from jax.experimental.pallas import tpu as pltpu
from jax.sharding import PartitionSpec as P

HD = 128
HCAP = 3
BLK = 128
YH, NZ, YL, NX, CORES = 4, 8, 2, 4, 2
HEADS = 4
TOK = 128
KEYS = HCAP * BLK + TOK
HALF = TOK // CORES
GROUPS = 4
PART = HALF // GROUPS
WIDTH = HEADS * HD
COLS = 256
NEG = -1e30
SCALE = math.log2(math.e) / math.sqrt(HD)
Y_STEP = (0, 3, 1, 2)
Z_STEP = (0, 7, 1, 6, 2, 5, 3, 4)
MESH = pl.DeviceIdType.MESH
F32 = jnp.float32
BF16 = jnp.bfloat16


def at(yh, z, yl, x, core):
    return (yh * NZ + z, yl * (NX * CORES) + x * CORES + core)


def kernel(
    q_hbm, suffix_hbm, pool_hbm, w_hbm, count_ref, slots_ref, o_ref,
    q_ref, suffix_ref, pool_ref, kb, vb, qb, wb, acc, mx, ob, st, rob, rst, wt, ab, cb, rb, fb, fin,
    in_s, k_ss, k_rs, q_ss, q_rs, w_ss, w_rs, s_ss, s_rs, o_ss, o_rs, t_ss, t_rs, a_ss, a_rs,
    c_ss, c_rs, f_ss, f_rs,
):
    c_index = lax.axis_index("ctx")
    t_index = lax.axis_index("tp")
    yh, z = c_index // NZ, c_index % NZ
    yl, x, core = t_index // (NX * CORES), (t_index // CORES) % NX, t_index % CORES
    chip = yl * NX + x
    other = 1 - core
    z_right, z_left = at(yh, (z + 1) % NZ, yl, x, core), at(yh, (z + NZ - 1) % NZ, yl, x, core)
    y_right, y_left = at((yh + 1) % YH, z, yl, x, core), at((yh + YH - 1) % YH, z, yl, x, core)
    sibling = at(yh, z, yl, x, other)

    def remote(src, dst, send, recv, device):
        return pltpu.make_async_remote_copy(
            src_ref=src, dst_ref=dst, send_sem=send, recv_sem=recv,
            device_id=device, device_id_type=MESH,
        )

    y_tok = yl * 2 + x // 2
    step_in = (yh + YH - y_tok) % YH
    in_yl = (y_tok // 2 + ((step_in + 1) // 2 + 1)) % 2
    in_x = ((y_tok % 2 + 1 - step_in // 2) % 2) * 2 + x % 2

    g1 = (yl + yh // 2) % 2
    g0 = (x // 2 + yh % 2) % 2
    step_out = (1 - g1) * (2 - g0) + g1 * 3 * (1 - g0)
    out_y = (yh + step_out) % YH

    def out_device(to_core):
        return at(out_y, z, yh // 2, (yh % 2) * 2 + x % 2, to_core)

    barrier = pltpu.get_barrier_semaphore()
    greeted = [z_right, z_left, sibling]
    for step in range(1, YH):
        for to_core in range(CORES):
            greeted.append(at((yh + step) % YH, z, yl, x, to_core))
    for dy in range(YL):
        for dx in range(NX):
            if (dy, dx) != (0, 0):
                greeted.append(at(yh, z, (yl + dy) % YL, (x + dx) % NX, core))
    for from_core in range(CORES):
        greeted.append(at(y_tok, z, in_yl, in_x, from_core))
    for device in greeted:
        pl.semaphore_signal(barrier, inc=1, device_id=device, device_id_type=MESH)
    loads = [
        pltpu.make_async_copy(pool_hbm, pool_ref, in_s.at[0]),
        pltpu.make_async_copy(suffix_hbm, suffix_ref, in_s.at[1]),
        pltpu.make_async_copy(q_hbm, q_ref, in_s.at[2]),
        pltpu.make_async_copy(w_hbm, wb.at[0, 0], in_s.at[3]),
    ]
    for load in loads:
        load.start()

    def kv_copy(slot, which, part):
        buf = (kb, vb)[which]
        rows = pl.ds(part * (KEYS // 2), KEYS // 2)
        if slot == 7:
            source, device = (5, z_right) if which == 0 else (6, z_left)
        else:
            source, device = max(slot - 2, 0), z_right if slot % 2 else z_left
        return remote(
            buf.at[source, rows], buf.at[slot, rows],
            k_ss.at[slot, which, part], k_rs.at[slot, which, part], device,
        )

    def a_copy(slot, group, which):
        if slot == 7:
            source, device = (5, z_right) if which == 0 else (6, z_left)
            src, dst = ab.at[source, group, which], ab.at[slot, group, which]
        else:
            source, device = max(slot - 2, 0), z_right if slot % 2 else z_left
            src, dst = ab.at[source, group], ab.at[slot, group]
        return remote(
            src, dst, a_ss.at[slot, group, which], a_rs.at[slot, group, which], device
        )

    def y_copy(buf, ss, rs, slot, half):
        rows = pl.ds(half * (WIDTH // 2), WIDTH // 2)
        if slot == 3:
            source, device = (1, y_right) if half == 0 else (2, y_left)
        else:
            source, device = 0, y_right if slot == 1 else y_left
        return remote(
            buf.at[source, rows], buf.at[slot, rows], ss.at[slot, half], rs.at[slot, half], device
        )

    def q_copy(slot, half):
        return y_copy(qb, q_ss, q_rs, slot, half)

    def w_copy(slot, half):
        return y_copy(wb.at[0], w_ss, w_rs, slot, half)

    def sib_copy(slot):
        return remote(wb.at[0, slot], wb.at[1, slot], s_ss.at[slot], s_rs.at[slot], sibling)

    row_minus_col = lax.broadcasted_iota(jnp.int32, (2 * TOK, TOK), 0) % TOK - (
        lax.broadcasted_iota(jnp.int32, (2 * TOK, TOK), 1)
    )

    def y_step(slot):
        if isinstance(slot, int):
            return Y_STEP[slot]
        return (slot * 3 + (slot // 2) * 3 + (slot // 3) * 2) % YH

    def absorb(q_slots, slot, count):
        ones = []
        z_keys = []
        for i in range(count):
            z_key = (z + Z_STEP[slot + i]) % NZ
            z_keys.append(z_key)
            hits = count_ref[yh * NZ + z_key]
            for b in range(HCAP):
                ones.append(jnp.full((BLK, HD), jnp.where(b < hits, 1.0, 0.0), F32).astype(BF16))
            ones.append(jnp.ones((TOK, HD), BF16))
        ones = jnp.concatenate(ones, axis=0)
        keys = kb[slot : slot + count].reshape(count * KEYS, HD)
        values = jnp.concatenate([vb[slot : slot + count].reshape(count * KEYS, HD), ones], axis=1)
        blocks = [(q_slot, pair) for q_slot in q_slots for pair in range(HEADS // 2)]
        all_scores = [
            lax.dot_general(
                qb[q_slot, pair * 2 * TOK : (pair + 1) * 2 * TOK, :], keys,
                (((1,), (1,)), ((), ())), preferred_element_type=F32,
            )
            for q_slot, pair in blocks
        ]
        for (q_slot, pair), scores in zip(blocks, all_scores):
            rows = slice(pair * 2 * TOK, (pair + 1) * 2 * TOK)
            y_query = (yh + y_step(q_slot)) % YH
            parts = []
            for i in range(count):
                gap = ((y_query - yh) * NZ + z - z_keys[i]) * TOK
                parts.append(scores[:, i * KEYS : i * KEYS + HCAP * BLK])
                own = scores[:, i * KEYS + HCAP * BLK : (i + 1) * KEYS]
                parts.append(jnp.where(row_minus_col + gap >= 0, own, NEG))
            scores = jnp.concatenate(parts, axis=1)
            before = mx[q_slot, rows, :]
            now = jnp.maximum(before, jnp.max(scores, axis=1, keepdims=True))
            mx[q_slot, rows, :] = now
            fade = jnp.exp2((before - now) * SCALE)
            weights = jnp.exp2((scores - now[:, :1]) * SCALE).astype(BF16)
            mixed = jnp.dot(weights, values, preferred_element_type=F32)
            acc[q_slot, rows, :] = (
                acc[q_slot, rows, :] * jnp.concatenate([fade, fade], axis=1) + mixed
            )

    loads[0].wait()
    loads[1].wait()
    hits = count_ref[c_index]
    for b in range(HCAP):
        rows = slice(b * BLK, (b + 1) * BLK)
        kept = b < hits
        kb[0, rows, :] = pool_ref[0, jnp.where(kept, slots_ref[0, b], slots_ref[0, 0])]
        keep = jnp.full((BLK, HD), jnp.where(kept, 1.0, 0.0), F32).astype(BF16)
        vb[0, rows, :] = pool_ref[1, slots_ref[0, b]] * keep
    kb[0, HCAP * BLK :, :] = suffix_ref[0]
    vb[0, HCAP * BLK :, :] = suffix_ref[1]
    loads[2].wait()
    for head in range(HEADS):
        qb[0, head * TOK : (head + 1) * TOK, :] = q_ref[:, head * HD : (head + 1) * HD]
    pl.semaphore_wait(barrier, len(greeted))
    for which in range(2):
        for part in range(2):
            for slot in (1, 2):
                kv_copy(slot, which, part).start()
    for slot, half in ((1, 0), (2, 1), (1, 1), (2, 0)):
        q_copy(slot, half).start()
    loads[3].wait()
    sib_copy(0).start()

    @pl.loop(0, YH)
    def _(slot):
        mx[slot] = jnp.full((WIDTH, HD), NEG, F32)
        acc[slot] = jnp.zeros((WIDTH, 2 * HD), F32)

    def pass_on(slot):
        for which in range(2):
            for part in range(2):
                for s in (slot, slot + 1):
                    kv_copy(s, which, part).wait_recv()
                    if s + 2 < 7:
                        kv_copy(s + 2, which, part).start()
                    elif (s, which) in ((5, 0), (6, 1)):
                        kv_copy(7, which, part).start()

    absorb([0], 0, 1)
    pass_on(1)
    absorb([0], 1, 2)
    q_copy(1, 0).wait_recv()
    q_copy(3, 0).start()
    q_copy(2, 1).wait_recv()
    q_copy(3, 1).start()
    q_copy(1, 1).wait_recv()
    q_copy(2, 0).wait_recv()
    for slot, half in ((1, 0), (2, 1), (1, 1), (2, 0)):
        w_copy(slot, half).start()
    pass_on(3)

    absorb([1, 2], 0, 3)

    @pl.loop(0, 3)
    def _(slot):
        absorb([slot], 3, 2)

    pass_on(5)
    q_copy(3, 0).wait_recv()
    q_copy(3, 1).wait_recv()
    absorb([3], 0, 5)

    @pl.loop(0, 2)
    def _(pair):
        absorb([2 * pair, 2 * pair + 1], 5, 2)

    w_copy(1, 0).wait_recv()
    w_copy(3, 0).start()
    w_copy(2, 1).wait_recv()
    w_copy(3, 1).start()
    w_copy(1, 1).wait_recv()
    sib_copy(1).start()
    w_copy(2, 0).wait_recv()
    sib_copy(2).start()
    for which in range(2):
        for part in range(2):
            kv_copy(7, which, part).wait_recv()

    lane = lax.broadcasted_iota(jnp.int32, (TOK, HD), 1)

    def finish(slot):
        stats = jnp.ones((TOK, HD), F32)
        for head in range(HEADS):
            rows = slice(head * TOK, (head + 1) * TOK)
            total = acc[slot, rows, HD:]
            result = (acc[slot, rows, :HD] / total).astype(BF16)
            for to_core in range(CORES):
                for group in range(GROUPS):
                    row = to_core * HALF + group * PART
                    ob[slot, to_core, group, :, head * HD : (head + 1) * HD] = (
                        result[row : row + PART]
                    )
            stats = jnp.where(lane == head, mx[slot, rows, :] * SCALE, stats)
            stats = jnp.where(lane == 8 + head, total, stats)
        st[slot] = stats.T[:16, :]

    def o_copies(slot, which, group):
        to_core = (core, other)[which]
        device = at((yh + Y_STEP[slot]) % YH, z, yl, x, to_core)
        copies = []
        if group == 0:
            copies.append(
                remote(
                    st.at[slot], rst.at[which, slot],
                    t_ss.at[slot, which], t_rs.at[slot, which], device,
                )
            )
        copies.append(
            remote(
                ob.at[slot, to_core, group], rob.at[which, slot, group],
                o_ss.at[slot, which, group], o_rs.at[slot, which, group], device,
            )
        )
        return copies

    def all_o_copies(slots, group):
        return [
            copy
            for slot in slots
            for which in range(CORES)
            if (slot, which) != (0, 0)
            for copy in o_copies(slot, which, group)
        ]

    for pair in ((3, 1), (2, 0)):
        absorb(pair, 7, 1)
        for slot in pair:
            finish(slot)
            for copy in all_o_copies([slot], 0):
                copy.start()
    for group in range(1, GROUPS):
        for copy in all_o_copies((3, 1, 2, 0), group):
            copy.start()
    rst[0, 0] = st[0]
    rob[0, 0] = ob[0, core]
    w_copy(3, 0).wait_recv()
    w_copy(3, 1).wait_recv()
    sib_copy(3).start()

    for group in range(GROUPS):
        for copy in all_o_copies((3, 1, 2, 0), group):
            copy.wait_recv()
        if group == 0:
            shares = []
            for which in range(CORES):
                top = rst[which, 0, :8]
                for slot in range(1, YH):
                    top = jnp.maximum(top, rst[which, slot, :8])
                raw = [
                    rst[which, slot, 8:] * jnp.exp2(rst[which, slot, :8] - top)
                    for slot in range(YH)
                ]
                whole = raw[0] + raw[1] + raw[2] + raw[3]
                shares += [share / whole for share in raw]
            wt[...] = jnp.concatenate(shares + shares, axis=0).T
        share = wt[pl.ds(pl.multiple_of(core * HALF + group * PART, PART), PART), :]
        for which in range(CORES):
            for head in range(HEADS):
                columns = slice(head * HD, (head + 1) * HD)
                summed = jnp.zeros((PART, HD), F32)
                for slot in range(YH):
                    spot = (which * YH + slot) * 8 + head
                    summed += (
                        share[:, spot : spot + 1] * rob[which, slot, group, :, columns].astype(F32)
                    )
                ab[0, group, which, :, columns] = summed.astype(BF16)
        for slot in (1, 2):
            a_copy(slot, group, 0).start()

    def c_place(slot, w_slot):
        step = Y_STEP[w_slot]
        c1, c0 = ((1, 1), (0, 1), (0, 0), (1, 0))[step]
        z_tok = (z + Z_STEP[slot]) % NZ
        to_yl = (yh // 2 + c1) % 2
        to_x = ((yh % 2 + c0) % 2) * 2 + z_tok // 4
        return to_yl, to_x, z_tok % 4

    def c_copy(slot, w_slot):
        to_yl, to_x, spot = c_place(slot, w_slot)
        return remote(
            cb.at[slot, w_slot], rb.at[chip, spot],
            c_ss.at[slot, w_slot], c_rs.at[chip, spot], at(yh, z, to_yl, to_x, core),
        )

    def project(slot, count):
        left = [
            ab[slot : slot + count, :, which].reshape(count * HALF, WIDTH)
            for which in range(CORES)
        ]
        for w_slot in (3, 1, 2, 0):
            part = jnp.dot(left[0], wb[0, w_slot], preferred_element_type=F32)
            part += jnp.dot(left[1], wb[1, w_slot], preferred_element_type=F32)
            part = part.astype(BF16)
            for i in range(count):
                cb[slot + i, w_slot] = part[i * HALF : (i + 1) * HALF]
                to_yl, to_x, spot = c_place(slot + i, w_slot)
                here = to_yl * NX + to_x == chip

                @pl.when(here)
                def _():
                    rb[chip, spot] = part[i * HALF : (i + 1) * HALF]

                @pl.when(jnp.logical_not(here))
                def _():
                    c_copy(slot + i, w_slot).start()

    def pass_a(slot, group):
        for s in (slot, slot + 1):
            a_copy(s, group, 0).wait_recv()
            if s + 2 < 7:
                a_copy(s + 2, group, 0).start()
            else:
                a_copy(7, group, s - 5).start()

    def f_copy(spot):
        row = (spot % 2) * TOK + core * HALF
        return remote(
            fb.at[spot], fin.at[pl.ds(pl.multiple_of(row, HALF), HALF)],
            f_ss.at[spot], f_rs.at[spot % 2, core], out_device(spot // 2),
        )

    def reduce(slot):
        z_tok = (z + Z_STEP[slot]) % NZ
        spot = z_tok % 4

        @pl.when(z_tok // 4 == x % 2)
        def _():
            @pl.loop(0, YL * NX)
            def _(source):
                @pl.when(source != chip)
                def _():
                    remote(
                        cb.at[0, 0], rb.at[source, spot],
                        c_ss.at[0, 0], c_rs.at[source, spot], sibling,
                    ).wait_recv()

            summed = rb[0, spot].astype(F32)
            for source in range(1, YL * NX):
                summed += rb[source, spot].astype(F32)
            fb[spot] = summed.astype(BF16)
            f_copy(spot).start()

    for slot in range(YH):
        sib_copy(slot).wait_recv()
    pass_a(1, 0)
    project(0, 1)
    for group in range(1, GROUPS):
        pass_a(1, group)
    pass_a(3, 0)
    project(1, 2)
    for group in range(1, GROUPS):
        pass_a(3, group)
    pass_a(5, 0)
    project(3, 2)
    for group in range(1, GROUPS):
        pass_a(5, group)
    reduce(0)
    project(5, 2)
    for slot in range(1, 5):
        reduce(slot)
    for group in range(GROUPS):
        for which in range(2):
            a_copy(7, group, which).wait_recv()
    project(7, 1)
    for slot in range(5, NZ):
        reduce(slot)

    for spot in range(2):
        for from_core in range(CORES):
            row = spot * TOK + from_core * HALF
            remote(
                fb.at[0], fin.at[row : row + HALF], f_ss.at[0], f_rs.at[spot, from_core], sibling
            ).wait_recv()
    o_ref[...] = fin[...]

    for which in range(2):
        for slot in range(1, NZ):
            for part in range(2):
                kv_copy(slot, which, part).wait_send()
    for group in range(GROUPS):
        for slot in range(1, NZ - 1):
            a_copy(slot, group, 0).wait_send()
        for which in range(2):
            a_copy(NZ - 1, group, which).wait_send()
        for copy in all_o_copies(range(YH), group):
            copy.wait_send()
    for slot in range(1, YH):
        for half in range(2):
            q_copy(slot, half).wait_send()
            w_copy(slot, half).wait_send()
    for slot in range(YH):
        sib_copy(slot).wait_send()
    for slot in range(NZ):
        for w_slot in range(YH):
            to_yl, to_x, _ = c_place(slot, w_slot)

            @pl.when(to_yl * NX + to_x != chip)
            def _():
                c_copy(slot, w_slot).wait_send()
    for spot in range(4):
        f_copy(spot).wait_send()


def body(queries, suffix_kv, cache_pool, hit_count, hit_slots, out_weight):
    vmem = pl.BlockSpec(memory_space=pltpu.VMEM)
    hbm = pl.BlockSpec(memory_space=pl.ANY)
    smem = pl.BlockSpec(memory_space=pltpu.SMEM)
    dma = pltpu.SemaphoreType.DMA
    return pl.pallas_call(
        kernel,
        out_shape=jax.ShapeDtypeStruct((2 * TOK, COLS), BF16),
        in_specs=[hbm] * 4 + [smem] * 2,
        out_specs=vmem,
        scratch_shapes=[
            pltpu.VMEM(queries.shape, BF16),
            pltpu.VMEM(suffix_kv.shape, BF16),
            pltpu.VMEM(cache_pool.shape, BF16),
            pltpu.VMEM((NZ, KEYS, HD), BF16),
            pltpu.VMEM((NZ, KEYS, HD), BF16),
            pltpu.VMEM((YH, WIDTH, HD), BF16),
            pltpu.VMEM((CORES, YH, WIDTH, COLS), BF16),
            pltpu.VMEM((YH, WIDTH, 2 * HD), F32),
            pltpu.VMEM((YH, WIDTH, HD), F32),
            pltpu.VMEM((YH, CORES, GROUPS, PART, WIDTH), BF16),
            pltpu.VMEM((YH, 16, TOK), F32),
            pltpu.VMEM((CORES, YH, GROUPS, PART, WIDTH), BF16),
            pltpu.VMEM((CORES, YH, 16, TOK), F32),
            pltpu.VMEM((TOK, HD), F32),
            pltpu.VMEM((NZ, GROUPS, CORES, PART, WIDTH), BF16),
            pltpu.VMEM((NZ, YH, HALF, COLS), BF16),
            pltpu.VMEM((YL * NX, 4, HALF, COLS), BF16),
            pltpu.VMEM((4, HALF, COLS), BF16),
            pltpu.VMEM((2 * TOK, COLS), BF16),
            dma((4,)),
            dma((NZ, 2, 2)), dma((NZ, 2, 2)),
            dma((YH, 2)), dma((YH, 2)),
            dma((YH, 2)), dma((YH, 2)),
            dma((YH,)), dma((YH,)),
            dma((YH, 2, GROUPS)), dma((YH, 2, GROUPS)),
            dma((YH, 2)), dma((YH, 2)),
            dma((NZ, GROUPS, 2)), dma((NZ, GROUPS, 2)),
            dma((NZ, YH)), dma((YL * NX, 4)),
            dma((4,)), dma((2, CORES)),
        ],
        compiler_params=pltpu.CompilerParams(
            collective_id=0, has_side_effects=True, vmem_limit_bytes=62 << 20
        ),
        cost_estimate=pl.CostEstimate(
            flops=6_000_000_000, bytes_accessed=1_000_000, transcendentals=8_400_000
        ),
        name="attention_and_projection",
    )(queries, suffix_kv, cache_pool, out_weight, hit_count, hit_slots)


def solution(mesh):
    placed = (
        P("ctx", "tp"),
        P(None, "ctx", "tp"),
        P(None, "ctx", None, "tp"),
        P(),
        P("ctx", None),
        P("tp", "ctx"),
    )
    return jax.shard_map(
        body, mesh=mesh, in_specs=placed, out_specs=P("tp", "ctx"), check_vma=False
    )
```
